32 devices in a mesh: grp: 4 (over z), seq: 8 (over y, x, core).
Axes of the slice: x: 2, y: 2, z: 4, core: 2. Of those that a mesh axis runs over, the one named last changes fastest.
Arguments:
- queries: bfloat16 [4096, 6144], P(('grp', 'seq')), may hold values from -64 to 64
- keys_values: bfloat16 [4096, 768], P(('grp', 'seq')), may hold values from -6 to 6
- selection: int32 [64, 32], P(('grp', 'seq')), may hold values from -1 to 63, as said below
- gate_logits: bfloat16 [3, 4096, 32], P(None, ('grp', 'seq')), may hold values from -6 to 6
- pos_weight: bfloat16 [64, 384], replicated, may hold values from -0.75 to 0.75
- compress_weight: bfloat16 [384, 384], replicated, may hold values from -0.3125 to 0.3125
Outputs:
- attended: bfloat16 [4096, 6144], P(('grp', 'seq'))
The draws below stay inside these ranges and needn't reach their ends.
Inputs may be any that keep to these rules, and one draw needn't show every extreme that they name: `selection`: A run is the 2 rows of one device; a segment is 16 consecutive rows. Row r lists, for each group, 16 distinct block numbers no greater than r, or -1 for unused entries. Within one group, the rows of a run list from each earlier segment exactly one block, and it lies in the run at the same place of that segment; from any other run of their own segment they list at most one block.
All inputs are finite; a program needn't handle non-finite values.
Results may differ from the reference program's by a relative error of at most 0.0055.
Values may be sent and summed in bfloat16 or wider, within the bound.
A program may use at most 128 MiB of HBM per device.

```python
import jax
import jax.numpy as jnp
from jax import lax

HEAD_DIM = 192
GROUPS = 2
GROUP_HEADS = 16
HEADS = 32
BLOCK = 64
TOP = 16
FAR_TOP = 8
WINDOW = 128
DEV_BLOCKS = 2
SEG_BLOCKS = 16
TOKENS = 4096
BLOCKS = 64


def base_pairs(key):
    inner = jax.random.fold_in(key, 7)
    return jnp.clip(jax.random.normal(inner, (TOKENS, GROUPS * 2 * HEAD_DIM)), -6.0, 6.0)


def draw_keys_values(key, part):
    return base_pairs(key).astype(jnp.bfloat16)


def draw_queries(key, part):
    query_key = jax.random.fold_in(key, 11)
    return jnp.clip(jax.random.normal(query_key, (TOKENS, HEADS * HEAD_DIM)), -6.0, 6.0).astype(jnp.bfloat16)


def shuffle_last(key, values):
    length = values.shape[-1]
    scores = jax.random.randint(key, values.shape, 0, 2 ** 16) * length + jnp.arange(length, dtype=jnp.int32)
    order = jnp.argsort(scores, axis=-1)
    return jnp.take_along_axis(values, order, axis=-1)


def draw_selection(key, part):
    segments = BLOCKS // SEG_BLOCKS
    devices = BLOCKS // DEV_BLOCKS
    runs = SEG_BLOCKS // DEV_BLOCKS
    far_len = DEV_BLOCKS * FAR_TOP
    near_each = TOP - FAR_TOP - 2
    near_len = DEV_BLOCKS * near_each
    near_take = min(near_len, runs)
    far_key, far_mix, peer_key, near_off, near_mix = jax.random.split(jax.random.fold_in(key, 3), 5)
    dev_ids = jnp.arange(devices, dtype=jnp.int32)
    dev_segment = dev_ids // runs
    dev_place = dev_ids % runs
    earlier = jnp.arange(segments - 1, dtype=jnp.int32)
    far_off = jax.random.randint(far_key, (devices, GROUPS, segments - 1), 0, DEV_BLOCKS)
    far_pool = earlier[None, None, :] * SEG_BLOCKS + dev_place[:, None, None] * DEV_BLOCKS + far_off
    far_pool = jnp.where(earlier[None, None, :] < dev_segment[:, None, None], far_pool, -1)
    far_pool = jnp.concatenate([far_pool, jnp.full((devices, GROUPS, far_len - (segments - 1)), -1, jnp.int32)], axis=2)
    far_pool = shuffle_last(far_mix, far_pool)
    far_blocks = jnp.transpose(far_pool.reshape(devices, GROUPS, DEV_BLOCKS, FAR_TOP), (0, 2, 1, 3)).reshape(BLOCKS, GROUPS, FAR_TOP)
    peers = jnp.arange(runs, dtype=jnp.int32)
    peer_raw = jax.random.randint(peer_key, (devices, GROUPS, runs), 0, 2 ** 16) * runs + peers
    peer_raw = jnp.where(peers[None, None, :] < dev_place[:, None, None], peer_raw, -1)
    peer_score, peer_pick = lax.top_k(peer_raw, near_take)
    peer_off = jax.random.randint(near_off, (devices, GROUPS, near_take), 0, DEV_BLOCKS)
    near_pool = dev_segment[:, None, None] * SEG_BLOCKS + peer_pick * DEV_BLOCKS + peer_off
    near_pool = jnp.where(peer_score >= 0, near_pool, -1)
    near_pool = jnp.concatenate([near_pool, jnp.full((devices, GROUPS, near_len - near_take), -1, jnp.int32)], axis=2)
    near_pool = shuffle_last(near_mix, near_pool)
    near_blocks = jnp.transpose(near_pool.reshape(devices, GROUPS, DEV_BLOCKS, near_each), (0, 2, 1, 3)).reshape(BLOCKS, GROUPS, near_each)
    query_ids = jnp.arange(BLOCKS, dtype=jnp.int32)
    previous = jnp.where(query_ids % DEV_BLOCKS >= 1, query_ids - 1, -1)
    local_pair = jnp.broadcast_to(jnp.stack([query_ids, previous], axis=1)[:, None, :], (BLOCKS, GROUPS, 2))
    listed = jnp.concatenate([far_blocks, local_pair, near_blocks], axis=2)
    return listed.reshape(BLOCKS, GROUPS * TOP).astype(jnp.int32)


def shard_levels(own_key, dims, cuts, low, largest):
    gain = 1.0
    for position, parts in cuts:
        steps = jax.random.uniform(jax.random.fold_in(jax.random.fold_in(own_key, 6), position), (parts,), jnp.float32, low / len(cuts), largest / len(cuts))
        gain = gain * jnp.repeat(jnp.exp(steps), dims[position] // parts).reshape((-1,) + (1,) * (len(dims) - 1 - position))
    return gain


def gaussian(own_key, extent, scale, most, cuts=(), kind=jnp.bfloat16):
    factor_of = shard_levels(own_key, extent, cuts, -0.22, 0.18) if cuts else 1.0
    entries = jax.random.normal(own_key, extent, jnp.float32) * scale * factor_of
    return jnp.minimum(jnp.maximum(entries, -most), most).astype(kind)


def setup_inputs(seed: int = 0) -> dict:
    key_list = jax.random.split(jax.random.key(seed), 7)
    return {
        "queries": draw_queries(jax.random.fold_in(key_list[6], 71), 0),
        "keys_values": draw_keys_values(jax.random.fold_in(key_list[6], 71), 0),
        "selection": draw_selection(jax.random.fold_in(key_list[6], 71), 0),
        "gate_logits": gaussian(key_list[3], (3, TOKENS, HEADS), 1.5, 6.0, ((1, 32),)),
        "pos_weight": gaussian(key_list[4], (BLOCK, 2 * HEAD_DIM), BLOCK ** -0.5, 0.75),
        "compress_weight": gaussian(key_list[5], (2 * HEAD_DIM, 2 * HEAD_DIM), (2 * HEAD_DIM) ** -0.5, 0.3125),
    }


NEG_FILL = -1e30


def attend(query_block, key_block, allowed, with_sink):
    head_dim = query_block.shape[-1]
    score_scale = head_dim ** -0.5
    scores = jnp.einsum("btghd,bgnd->bghtn", query_block.astype(jnp.float32), key_block[..., :head_dim].astype(jnp.float32)) * score_scale
    allowed_wide = allowed[:, :, None]
    scores = jnp.where(allowed_wide, scores, NEG_FILL)
    top_score = jnp.max(scores, axis=-1, keepdims=True)
    if with_sink:
        top_score = jnp.maximum(top_score, 0.0)
    weights = jnp.where(allowed_wide, jnp.exp(scores - top_score), 0.0)
    denominator = jnp.sum(weights, axis=-1, keepdims=True)
    if with_sink:
        denominator = denominator + jnp.exp(-top_score)
    rounded = weights.astype(jnp.bfloat16)
    blended = jnp.einsum("bghtn,bgnd->bghtd", rounded.astype(jnp.float32), key_block[..., head_dim:].astype(jnp.float32)) / denominator
    return jnp.transpose(blended, (0, 3, 1, 2, 4))


def compress_blocks(keys_values, pos_weight, compress_weight):
    block_count = keys_values.shape[0] // BLOCK
    grouped = keys_values.reshape(block_count, BLOCK, GROUPS, 2 * HEAD_DIM).astype(jnp.float32)
    pooled = jnp.sum(grouped * pos_weight.astype(jnp.float32)[None, :, None, :], axis=1).astype(jnp.bfloat16)
    mapped = jnp.dot(pooled.reshape(block_count * GROUPS, 2 * HEAD_DIM), compress_weight, preferred_element_type=jnp.float32)
    return mapped.astype(jnp.bfloat16).reshape(block_count, GROUPS, 2 * HEAD_DIM)


def reference(queries, keys_values, selection, gate_logits, pos_weight, compress_weight):
    summaries = jnp.transpose(compress_blocks(keys_values, pos_weight, compress_weight), (1, 0, 2))[None]
    padded = jnp.concatenate([jnp.zeros((WINDOW, GROUPS * 2 * HEAD_DIM), keys_values.dtype), keys_values], axis=0)
    block_view = keys_values.reshape(BLOCKS, BLOCK, GROUPS, 2 * HEAD_DIM)
    block_ends = jnp.arange(BLOCKS, dtype=jnp.int32) * BLOCK + BLOCK - 1
    group_ids = jnp.arange(GROUPS, dtype=jnp.int32)[:, None]
    offsets = jnp.arange(BLOCK, dtype=jnp.int32)
    near_offsets = jnp.arange(WINDOW + BLOCK, dtype=jnp.int32)

    def one_block(block_index):
        first_row = block_index * BLOCK
        query_block = lax.dynamic_slice_in_dim(queries, first_row, BLOCK, 0).reshape(1, BLOCK, GROUPS, GROUP_HEADS, HEAD_DIM)
        positions = first_row + offsets
        allowed_comp = (block_ends[None, :] <= positions[:, None])[None, None]
        compressed_branch = attend(query_block, summaries, allowed_comp, True)
        picked = lax.dynamic_slice_in_dim(selection, block_index, 1, 0).reshape(GROUPS, TOP)
        clipped = jnp.maximum(picked, 0)
        chosen = block_view[clipped, :, group_ids, :].reshape(1, GROUPS, TOP * BLOCK, 2 * HEAD_DIM)
        key_positions = (clipped[:, :, None] * BLOCK + offsets).reshape(GROUPS, TOP * BLOCK)
        live_keys = jnp.repeat(picked >= 0, BLOCK, axis=1)
        allowed_sel = (live_keys[:, None, :] & (key_positions[:, None, :] <= positions[None, :, None]))[None]
        selected_branch = attend(query_block, chosen, allowed_sel, False)
        nearby = lax.dynamic_slice_in_dim(padded, first_row, WINDOW + BLOCK, 0).reshape(WINDOW + BLOCK, GROUPS, 2 * HEAD_DIM)
        nearby = jnp.transpose(nearby, (1, 0, 2))[None]
        near_positions = first_row - WINDOW + near_offsets
        allowed_win = ((near_positions[None, :] <= positions[:, None]) & (near_positions[None, :] > positions[:, None] - WINDOW) & (near_positions[None, :] >= 0))[None, None]
        window_branch = attend(query_block, nearby, allowed_win, False)
        gate_values = jax.nn.sigmoid(lax.dynamic_slice_in_dim(gate_logits, first_row, BLOCK, 1).astype(jnp.float32)).reshape(3, 1, BLOCK, GROUPS, GROUP_HEADS, 1)
        attended = gate_values[0] * compressed_branch + gate_values[1] * selected_branch + gate_values[2] * window_branch
        return attended.reshape(BLOCK, HEADS * HEAD_DIM).astype(jnp.bfloat16)

    outputs = lax.map(one_block, jnp.arange(BLOCKS, dtype=jnp.int32))
    return outputs.reshape(TOKENS, HEADS * HEAD_DIM)
```

```python
import functools
import math

import jax
import jax.numpy as jnp
from jax import lax
from jax.experimental import pallas as pl
from jax.experimental.pallas import tpu as pltpu
from jax.sharding import PartitionSpec as P

HEAD_DIM = 192
GROUPS = 2
GROUP_HEADS = 16
HEADS = 32
BLOCK = 64
TOP = 16
WINDOW = 128
PAIR = 2 * HEAD_DIM
WIDE = 256
CHUNK = 4
PAIRS = GROUP_HEADS // 2
NEG_FILL = -1e30
EXP2_SCALE = HEAD_DIM ** (-0.5) * math.log2(math.e)
FAR_POS = 1 << 30


def exchange(grp_count, seq_count, kv_ref, sel_ref, pos_ref, map_ref, pool_ref, prev_ref, sums_ref,
             lists, staged, mine, list_send, list_recv, data_send, data_recv, sum_send, sum_recv,
             prev_send, prev_recv):
    grp = lax.axis_index("grp")
    seq = lax.axis_index("seq")
    last = seq_count - 1
    first_block = (grp * seq_count + seq) * 2

    barrier = pltpu.get_barrier_semaphore()

    def near(place):
        return (grp, place)

    def far(segment):
        return (segment, seq)

    def greet(where):
        pl.semaphore_signal(barrier, inc=1, device_id=where, device_id_type=pl.DeviceIdType.MESH)

    def each(low, high, body):
        def step(i, carry):
            body(i)
            return carry

        lax.fori_loop(low, high, step, 0)

    def others(count, me, body):
        each(0, me, body)
        each(me + 1, count, body)

    others(seq_count, seq, lambda i: greet(near(i)))
    others(grp_count, grp, lambda i: greet(far(i)))
    tail_out = jnp.logical_and(seq == last, grp < grp_count - 1)
    tail_in = jnp.logical_and(seq == 0, grp > 0)

    @pl.when(tail_out)
    def _():
        greet((grp + 1, 0))

    @pl.when(tail_in)
    def _():
        greet((grp - 1, last))

    extra = tail_out.astype(jnp.int32) + tail_in.astype(jnp.int32)
    pl.semaphore_wait(barrier, seq_count + grp_count - 2 + extra)

    def remote(src, dst, send, recv, where):
        return pltpu.make_async_remote_copy(
            src_ref=src, dst_ref=dst, send_sem=send, recv_sem=recv, device_id=where,
            device_id_type=pl.DeviceIdType.MESH)

    def list_copy(theirs, own, where):
        return remote(sel_ref, lists.at[own], list_send.at[theirs], list_recv.at[own], where)

    each(0, grp, lambda i: list_copy(seq_count + i, seq_count + grp, far(i)).start())
    each(0, seq, lambda i: list_copy(i, seq, near(i)).start())

    def prev_copy(where):
        return remote(kv_ref, prev_ref, prev_send, prev_recv, where)

    @pl.when(seq < last)
    def _():
        prev_copy((grp, seq + 1)).start()

    @pl.when(tail_out)
    def _():
        prev_copy((grp + 1, 0)).start()

    rows = []
    for b in range(2):
        for g in range(GROUPS):
            part = kv_ref[b * BLOCK:(b + 1) * BLOCK, g * PAIR:(g + 1) * PAIR].astype(jnp.float32)
            rows.append(jnp.sum(part * pos_ref[...].astype(jnp.float32), axis=0, keepdims=True))
    pooled = jnp.concatenate(rows + [jnp.zeros((4, PAIR), jnp.float32)], axis=0).astype(jnp.bfloat16)
    mapped = jnp.dot(pooled, map_ref[...], preferred_element_type=jnp.float32)
    packed = jnp.concatenate(
        [mapped[0:4, c * 128:(c + 1) * 128] for c in range(3)] + [jnp.zeros((4, 128), jnp.float32)], axis=0)
    mine[...] = packed.astype(jnp.bfloat16)
    sums_ref[seq, grp] = mine[...]

    def column_copy(theirs, own, where):
        return remote(mine, sums_ref.at[seq, grp], sum_send.at[theirs], sum_recv.at[own], where)

    others(grp_count, grp, lambda i: column_copy(seq_count + i, seq_count + grp, far(i)).start())

    def data_copy(theirs, own, where):
        return remote(staged.at[theirs], pool_ref.at[own], data_send.at[theirs], data_recv.at[own], where)

    def answer(slot, own, where):
        list_copy(slot, slot, where).wait_recv()
        hit = jnp.where(lists[slot] == first_block + 1, 1.0, 0.0)
        for g in range(GROUPS):
            second = jnp.max(hit[:, g * TOP:(g + 1) * TOP], axis=(0, 1), keepdims=True)
            cols = pl.ds(g * PAIR, PAIR)
            low = kv_ref[0:BLOCK, cols].astype(jnp.float32)
            high = kv_ref[BLOCK:2 * BLOCK, cols].astype(jnp.float32)
            pick = jnp.broadcast_to(second, (BLOCK, PAIR)) > 0.5
            staged[slot, :, cols] = jnp.where(pick, high, low).astype(jnp.bfloat16)
        data_copy(slot, own, where).start()

    each(grp + 1, grp_count, lambda i: answer(seq_count + i, seq_count + grp, far(i)))
    each(seq + 1, seq_count, lambda i: answer(i, seq, near(i)))

    others(grp_count, grp, lambda i: column_copy(seq_count + i, seq_count + i, far(i)).wait_recv())

    def row_copy(theirs, own, where):
        return remote(sums_ref.at[seq], sums_ref.at[own], sum_send.at[theirs], sum_recv.at[own], where)

    others(seq_count, seq, lambda i: row_copy(i, seq, near(i)).start())

    def row_wait(i):
        remote(sums_ref.at[seq], sums_ref.at[i], sum_send.at[i], sum_recv.at[i], near(i)).wait_recv()

    others(seq_count, seq, row_wait)

    each(0, grp, lambda i: data_copy(seq_count + i, seq_count + i, far(i)).wait_recv())
    each(0, seq, lambda i: data_copy(i, i, near(i)).wait_recv())

    @pl.when(jnp.logical_or(seq > 0, grp > 0))
    def _():
        prev_copy(far(grp)).wait_recv()

    @pl.when(jnp.logical_or(seq < last, grp < grp_count - 1))
    def _():
        prev_copy(far(grp)).wait_send()

    each(0, grp, lambda i: list_copy(seq_count + i, seq_count + i, far(i)).wait_send())
    each(0, seq, lambda i: list_copy(i, i, near(i)).wait_send())
    each(grp + 1, grp_count, lambda i: data_copy(seq_count + i, seq_count + i, far(i)).wait_send())
    each(seq + 1, seq_count, lambda i: data_copy(i, i, near(i)).wait_send())
    others(grp_count, grp, lambda i: column_copy(seq_count + i, seq_count + i, far(i)).wait_send())
    others(seq_count, seq, lambda i: row_copy(i, seq, near(i)).wait_send())


def run_exchange(keys_values, selection, pos_weight, compress_weight):
    grp_count = lax.axis_size("grp")
    seq_count = lax.axis_size("seq")
    slots = grp_count + seq_count
    vmem = pl.BlockSpec(memory_space=pltpu.VMEM)
    dma = pltpu.SemaphoreType.DMA((slots,))
    return pl.pallas_call(
        functools.partial(exchange, grp_count, seq_count),
        out_shape=(
            jax.ShapeDtypeStruct((slots, BLOCK, GROUPS * PAIR), jnp.bfloat16),
            jax.ShapeDtypeStruct(keys_values.shape, jnp.bfloat16),
            jax.ShapeDtypeStruct((seq_count, grp_count, 16, 128), jnp.bfloat16),
        ),
        in_specs=[vmem] * 4,
        out_specs=(pl.BlockSpec(memory_space=pl.ANY), pl.BlockSpec(memory_space=pl.ANY), vmem),
        scratch_shapes=[
            pltpu.VMEM((slots,) + selection.shape, jnp.int32),
            pltpu.VMEM((slots, BLOCK, GROUPS * PAIR), jnp.bfloat16),
            pltpu.VMEM((16, 128), jnp.bfloat16),
            dma, dma, dma, dma, dma, dma,
            pltpu.SemaphoreType.DMA,
            pltpu.SemaphoreType.DMA,
        ],
        compiler_params=pltpu.CompilerParams(
            collective_id=0, has_side_effects=True, vmem_limit_bytes=32 << 20),
    )(keys_values, selection, pos_weight, compress_weight)


def spread(pair):
    lane = lax.broadcasted_iota(jnp.int32, (pair.shape[0], WIDE), 1)
    low = pair[:, 0:WIDE].astype(jnp.float32)
    high = pair[:, PAIR - WIDE:PAIR].astype(jnp.float32)
    key_even = jnp.where(lane < HEAD_DIM, low, 0.0)
    key_odd = jnp.where(lane >= WIDE - HEAD_DIM, pltpu.roll(low, WIDE - HEAD_DIM, 1), 0.0)
    value_even = jnp.where(lane < HEAD_DIM, pltpu.roll(high, HEAD_DIM, 1),
                           jnp.where(lane == HEAD_DIM, 1.0, 0.0))
    value_odd = jnp.where(lane >= WIDE - HEAD_DIM, high, jnp.where(lane == 0, 1.0, 0.0))
    return [x.astype(jnp.bfloat16) for x in (key_even, key_odd, value_even, value_odd)]


def branch(query_rows, keys, values, biases, with_sink, ones_lane):
    heads = query_rows.shape[0] // BLOCK
    scores = []
    for key, bias in zip(keys, biases):
        raw = lax.dot_general(query_rows, key, (((1,), (1,)), ((), ())), preferred_element_type=jnp.float32)
        scores.append((raw.reshape(heads, BLOCK, raw.shape[1]) + bias[None]).reshape(raw.shape))
    top = functools.reduce(jnp.maximum, [jnp.max(s, axis=1, keepdims=True) for s in scores])
    if with_sink:
        top = jnp.maximum(top, 0.0)
    total = None
    for score, value in zip(scores, values):
        weights = jnp.exp2((score - top) * EXP2_SCALE).astype(jnp.bfloat16)
        part = jnp.dot(weights, value, preferred_element_type=jnp.float32)
        total = part if total is None else total + part
    below = total[:, ones_lane:ones_lane + 1]
    if with_sink:
        below = below + jnp.exp2(-top * EXP2_SCALE)
    return total, below


def attend(grp_count, seq_count, sel_ref, q_ref, kv_ref, pool_ref, prev_ref, sums_ref, gate_ref,
           out_ref, chosen, nearby, far_sums, acc, picks, spots):
    slots = grp_count + seq_count
    grp = lax.axis_index("grp")
    seq = lax.axis_index("seq")
    g = pl.program_id(0)
    b = pl.program_id(1)
    run = grp * seq_count + seq
    row_block = run * 2 + b
    cols = pl.ds(pl.multiple_of(g * PAIR, 128), PAIR)
    halves = PAIRS // 4

    @pl.when(b == 0)
    def _():
        def fill(slot, carry):
            for i, x in enumerate(spread(pool_ref[slot, :, cols])):
                chosen[i, slot] = x
            return carry

        lax.fori_loop(0, seq, fill, 0)
        lax.fori_loop(seq_count, seq_count + grp, fill, 0)
        own = spread(kv_ref[:, cols])
        before = spread(jnp.where(run > 0, prev_ref[:, cols], jnp.zeros_like(prev_ref[:, cols])))
        for i in range(4):
            chosen[i, slots] = own[i][0:BLOCK]
            chosen[i, slots + 1] = own[i][BLOCK:2 * BLOCK]
            nearby[i, 0:WINDOW] = before[i]
            nearby[i, WINDOW:2 * WINDOW] = own[i]
        for i, x in enumerate(spread(sums_ref[0])):
            far_sums[i] = x

    seg_blocks = 2 * seq_count

    def scan(i, count):
        block = sel_ref[b, g * TOP + i]
        segment = block // seg_blocks
        place = (block - segment * seg_blocks) // 2
        here = jnp.logical_and(segment == grp, place == seq)
        slot = jnp.where(here, slots + (block & 1), jnp.where(segment == grp, place, seq_count + segment))

        @pl.when(block >= 0)
        def _():
            picks[count] = slot
            spots[count] = block * BLOCK

        return count + jnp.where(block >= 0, 1, 0)

    for i in range(TOP):
        picks[i] = slots + b
        spots[i] = FAR_POS
    count = lax.fori_loop(0, TOP, scan, jnp.int32(0))

    @pl.when(count < TOP)
    def _():
        def blank(i, carry):
            picks[i] = slots + b
            spots[i] = FAR_POS
            return carry

        lax.fori_loop(count, TOP, blank, 0)

    token = row_block * BLOCK + lax.broadcasted_iota(jnp.int32, (BLOCK, 1), 0)

    def bias_of(allowed):
        return jnp.where(allowed, 0.0, NEG_FILL)

    key_pos = run * 2 * BLOCK - WINDOW + lax.broadcasted_iota(jnp.int32, (BLOCK, 2 * WINDOW), 1)
    near_bias = bias_of((key_pos <= token) & (key_pos > token - WINDOW) & (key_pos >= 0))
    all_blocks = sums_ref.shape[1]
    block_end = lax.broadcasted_iota(jnp.int32, (BLOCK, all_blocks), 1) * BLOCK + BLOCK - 1
    sums_bias = bias_of(block_end <= token)

    gates = []
    for i in range(3):
        full = 1.0 / (1.0 + jnp.exp(-gate_ref[i].astype(jnp.float32)))
        gates.append(jnp.where(g == 0, full[:, 0:GROUP_HEADS], full[:, GROUP_HEADS:HEADS]))

    def rows_of(half, parity):
        starts = [(half * 4 + j) * PAIR + parity * (PAIR - WIDE) for j in range(4)]
        return jnp.concatenate([q_ref[:, s:s + WIDE] for s in starts], axis=0)

    def gate_of(i, half, parity):
        heads = [2 * (half * 4 + j) + parity for j in range(4)]
        return jnp.concatenate([gates[i][:, h:h + 1] for h in heads], axis=0)

    ones_lane = (HEAD_DIM, 0)
    for half in range(halves):
        for parity in range(2):
            rows = rows_of(half, parity)
            near_total, near_below = branch(
                rows, [nearby[parity]], [nearby[2 + parity]], [near_bias], False, ones_lane[parity])
            sums_total, sums_below = branch(
                rows, [far_sums[parity]], [far_sums[2 + parity]], [sums_bias], True, ones_lane[parity])
            acc[half, parity] = (near_total * (gate_of(2, half, parity) / near_below)
                                 + sums_total * (gate_of(0, half, parity) / sums_below))

    lane = lax.broadcasted_iota(jnp.int32, (BLOCK, CHUNK * BLOCK), 1)
    half_lane = lax.broadcasted_iota(jnp.int32, (BLOCK, 128), 1) < 64

    def selected(chunks):
        biases = []
        for c in range(chunks):
            base = jnp.full(lane.shape, spots[c * CHUNK], jnp.int32)
            for j in range(1, CHUNK):
                base = jnp.where(lane >= j * BLOCK, spots[c * CHUNK + j], base)
            biases.append(bias_of(base + (lane & (BLOCK - 1)) <= token))
        for half in range(halves):
            both = []
            for parity in range(2):
                def take(which):
                    return [
                        jnp.concatenate([chosen[which, picks[c * CHUNK + j]] for j in range(CHUNK)], axis=0)
                        for c in range(chunks)
                    ]

                total, below = branch(
                    rows_of(half, parity), take(parity), take(2 + parity), biases, False, ones_lane[parity])
                both.append(acc[half, parity] + total * (gate_of(1, half, parity) / below))
            for j in range(4):
                even = both[0][j * BLOCK:(j + 1) * BLOCK]
                odd = both[1][j * BLOCK:(j + 1) * BLOCK]
                start = (half * 4 + j) * PAIR
                out_ref[:, start:start + 128] = even[:, 0:128].astype(jnp.bfloat16)
                out_ref[:, start + 128:start + 256] = jnp.where(
                    half_lane, even[:, 128:256], odd[:, 0:128]).astype(jnp.bfloat16)
                out_ref[:, start + 256:start + 384] = odd[:, 128:256].astype(jnp.bfloat16)

    for chunks in range(1, TOP // CHUNK + 1):
        low = 0 if chunks == 1 else (chunks - 1) * CHUNK + 1

        @pl.when(jnp.logical_and(count >= low, count <= chunks * CHUNK))
        def _():
            selected(chunks)


def run_attend(selection, queries, keys_values, pool, prev, sums, gate_logits):
    grp_count = lax.axis_size("grp")
    seq_count = lax.axis_size("seq")
    slots = grp_count + seq_count
    all_blocks = sums.shape[1]

    def whole(x):
        return pl.BlockSpec(x.shape, lambda g, b, *_: (0,) * x.ndim)

    group_cols = GROUP_HEADS * HEAD_DIM
    return pl.pallas_call(
        functools.partial(attend, grp_count, seq_count),
        out_shape=jax.ShapeDtypeStruct(queries.shape, jnp.bfloat16),
        grid_spec=pltpu.PrefetchScalarGridSpec(
            num_scalar_prefetch=1,
            grid=(GROUPS, 2),
            in_specs=[
                pl.BlockSpec((BLOCK, group_cols), lambda g, b, *_: (b, g)),
                whole(keys_values), whole(pool), whole(prev),
                pl.BlockSpec((1, all_blocks, PAIR), lambda g, b, *_: (g, 0, 0)),
                pl.BlockSpec((3, BLOCK, HEADS), lambda g, b, *_: (0, b, 0)),
            ],
            out_specs=pl.BlockSpec((BLOCK, group_cols), lambda g, b, *_: (b, g)),
            scratch_shapes=[
                pltpu.VMEM((4, slots + 2, BLOCK, WIDE), jnp.bfloat16),
                pltpu.VMEM((4, 2 * WINDOW, WIDE), jnp.bfloat16),
                pltpu.VMEM((4, all_blocks, WIDE), jnp.bfloat16),
                pltpu.VMEM((PAIRS // 4, 2, 4 * BLOCK, WIDE), jnp.float32),
                pltpu.SMEM((TOP,), jnp.int32),
                pltpu.SMEM((TOP,), jnp.int32),
            ],
        ),
        compiler_params=pltpu.CompilerParams(vmem_limit_bytes=48 << 20),
    )(selection, queries, keys_values, pool, prev, sums, gate_logits)


def shards(queries, keys_values, selection, gate_logits, pos_weight, compress_weight):
    grp_count = lax.axis_size("grp")
    seq_count = lax.axis_size("seq")
    pool, prev, packed = run_exchange(keys_values, selection, pos_weight, compress_weight)
    sums = packed[:, :, :12].reshape(seq_count, grp_count, 3, 2, GROUPS, 128)
    sums = jnp.transpose(sums, (4, 1, 0, 3, 2, 5)).reshape(GROUPS, 2 * seq_count * grp_count, PAIR)
    return run_attend(selection, queries, keys_values, pool, prev, sums, gate_logits)


def solution(mesh):
    in_specs = (
        P(("grp", "seq"), None),
        P(("grp", "seq"), None),
        P(("grp", "seq"), None),
        P(None, ("grp", "seq"), None),
        P(),
        P(),
    )
    out_specs = P(("grp", "seq"), None)
    return jax.shard_map(shards, mesh=mesh, in_specs=in_specs, out_specs=out_specs, check_vma=False)
```

```python
import functools
import math

import jax
import jax.numpy as jnp
from jax import lax
from jax.experimental import pallas as pl
from jax.experimental.pallas import tpu as pltpu
from jax.sharding import PartitionSpec as P

HEAD_DIM = 192
GROUPS = 2
GROUP_HEADS = 16
HEADS = 32
BLOCK = 64
TOP = 16
WINDOW = 128
PAIR = 2 * HEAD_DIM
WIDE = 256
CHUNK = 4
PAIRS = GROUP_HEADS // 2
SINK_ROWS = 64
PARTS = 2
PART_ROWS = GROUP_HEADS * BLOCK // PARTS
NEG_FILL = -1e30
EXP2_SCALE = HEAD_DIM ** (-0.5) * math.log2(math.e)
FAR_POS = 1 << 30


def exchange(grp_count, seq_count, kv_in, sel_in, pos_in, map_in, pool_ref, prev_ref, sums_ref,
             kv_ref, sel_ref, pos_ref, map_ref, load_sems, lists, staged, mine, list_send, list_recv, data_send, data_recv, sum_send, sum_recv,
             prev_send, prev_recv):
    grp = lax.axis_index("grp")
    seq = lax.axis_index("seq")
    last = seq_count - 1
    first_block = (grp * seq_count + seq) * 2

    loads = [
        pltpu.make_async_copy(src, dst, load_sems.at[i])
        for i, (src, dst) in enumerate(
            ((sel_in, sel_ref), (kv_in, kv_ref), (pos_in, pos_ref), (map_in, map_ref)))
    ]
    for load in loads:
        load.start()

    barrier = pltpu.get_barrier_semaphore()

    def near(place):
        return (grp, place)

    def far(segment):
        return (segment, seq)

    def greet(where):
        pl.semaphore_signal(barrier, inc=1, device_id=where, device_id_type=pl.DeviceIdType.MESH)

    def each(low, high, body):
        def step(i, carry):
            body(i)
            return carry

        lax.fori_loop(low, high, step, 0)

    def others(count, me, body):
        each(0, me, body)
        each(me + 1, count, body)

    others(seq_count, seq, lambda i: greet(near(i)))
    others(grp_count, grp, lambda i: greet(far(i)))
    tail_out = jnp.logical_and(seq == last, grp < grp_count - 1)
    tail_in = jnp.logical_and(seq == 0, grp > 0)

    @pl.when(tail_out)
    def _():
        greet((grp + 1, 0))

    @pl.when(tail_in)
    def _():
        greet((grp - 1, last))

    extra = tail_out.astype(jnp.int32) + tail_in.astype(jnp.int32)
    pl.semaphore_wait(barrier, seq_count + grp_count - 2 + extra)
    for load in loads:
        load.wait()

    def remote(src, dst, send, recv, where):
        return pltpu.make_async_remote_copy(
            src_ref=src, dst_ref=dst, send_sem=send, recv_sem=recv, device_id=where,
            device_id_type=pl.DeviceIdType.MESH)

    def list_copy(theirs, own, where):
        return remote(sel_ref, lists.at[own], list_send.at[theirs], list_recv.at[own], where)

    each(0, grp, lambda i: list_copy(seq_count + i, seq_count + grp, far(i)).start())
    each(0, seq, lambda i: list_copy(i, seq, near(i)).start())

    def prev_copy(where):
        return remote(kv_ref, prev_ref, prev_send, prev_recv, where)

    @pl.when(seq < last)
    def _():
        prev_copy((grp, seq + 1)).start()

    @pl.when(tail_out)
    def _():
        prev_copy((grp + 1, 0)).start()

    rows = []
    for b in range(2):
        for g in range(GROUPS):
            part = kv_ref[b * BLOCK:(b + 1) * BLOCK, g * PAIR:(g + 1) * PAIR].astype(jnp.float32)
            rows.append(jnp.sum(part * pos_ref[...].astype(jnp.float32), axis=0, keepdims=True))
    pooled = jnp.concatenate(rows + [jnp.zeros((4, PAIR), jnp.float32)], axis=0).astype(jnp.bfloat16)
    mapped = jnp.dot(pooled, map_ref[...], preferred_element_type=jnp.float32)
    packed = jnp.concatenate(
        [mapped[0:4, c * 128:(c + 1) * 128] for c in range(3)] + [jnp.zeros((4, 128), jnp.float32)], axis=0)
    mine[...] = packed.astype(jnp.bfloat16)
    sums_ref[seq, grp] = mine[...]

    def column_copy(theirs, own, where):
        return remote(mine, sums_ref.at[seq, grp], sum_send.at[theirs], sum_recv.at[own], where)

    others(grp_count, grp, lambda i: column_copy(seq_count + i, seq_count + grp, far(i)).start())

    def data_copy(theirs, own, where):
        return remote(staged.at[theirs], pool_ref.at[own], data_send.at[theirs], data_recv.at[own], where)

    def answer(slot, own, where):
        list_copy(slot, slot, where).wait_recv()
        hit = jnp.where(lists[slot] == first_block + 1, 1.0, 0.0)
        for g in range(GROUPS):
            second = jnp.max(hit[:, g * TOP:(g + 1) * TOP], axis=(0, 1), keepdims=True)
            cols = pl.ds(g * PAIR, PAIR)
            low = kv_ref[0:BLOCK, cols].astype(jnp.float32)
            high = kv_ref[BLOCK:2 * BLOCK, cols].astype(jnp.float32)
            pick = jnp.broadcast_to(second, (BLOCK, PAIR)) > 0.5
            staged[slot, :, cols] = jnp.where(pick, high, low).astype(jnp.bfloat16)
        data_copy(slot, own, where).start()

    each(grp + 1, grp_count, lambda i: answer(seq_count + i, seq_count + grp, far(i)))
    each(seq + 1, seq_count, lambda i: answer(i, seq, near(i)))

    others(grp_count, grp, lambda i: column_copy(seq_count + i, seq_count + i, far(i)).wait_recv())

    def row_copy(theirs, own, where):
        return remote(sums_ref.at[seq], sums_ref.at[own], sum_send.at[theirs], sum_recv.at[own], where)

    others(seq_count, seq, lambda i: row_copy(i, seq, near(i)).start())

    def row_wait(i):
        remote(sums_ref.at[seq], sums_ref.at[i], sum_send.at[i], sum_recv.at[i], near(i)).wait_recv()

    others(seq_count, seq, row_wait)

    each(0, grp, lambda i: data_copy(seq_count + i, seq_count + i, far(i)).wait_recv())
    each(0, seq, lambda i: data_copy(i, i, near(i)).wait_recv())

    @pl.when(jnp.logical_or(seq > 0, grp > 0))
    def _():
        prev_copy(far(grp)).wait_recv()

    @pl.when(jnp.logical_or(seq < last, grp < grp_count - 1))
    def _():
        prev_copy(far(grp)).wait_send()

    each(0, grp, lambda i: list_copy(seq_count + i, seq_count + i, far(i)).wait_send())
    each(0, seq, lambda i: list_copy(i, i, near(i)).wait_send())
    each(grp + 1, grp_count, lambda i: data_copy(seq_count + i, seq_count + i, far(i)).wait_send())
    each(seq + 1, seq_count, lambda i: data_copy(i, i, near(i)).wait_send())
    others(grp_count, grp, lambda i: column_copy(seq_count + i, seq_count + i, far(i)).wait_send())
    others(seq_count, seq, lambda i: row_copy(i, seq, near(i)).wait_send())


def run_exchange(keys_values, selection, pos_weight, compress_weight):
    grp_count = lax.axis_size("grp")
    seq_count = lax.axis_size("seq")
    slots = grp_count + seq_count
    vmem = pl.BlockSpec(memory_space=pltpu.VMEM)
    dma = pltpu.SemaphoreType.DMA((slots,))
    return pl.pallas_call(
        functools.partial(exchange, grp_count, seq_count),
        out_shape=(
            jax.ShapeDtypeStruct((slots, BLOCK, GROUPS * PAIR), jnp.bfloat16),
            jax.ShapeDtypeStruct(keys_values.shape, jnp.bfloat16),
            jax.ShapeDtypeStruct((seq_count, grp_count, 16, 128), jnp.bfloat16),
        ),
        in_specs=[pl.BlockSpec(memory_space=pl.ANY)] * 4,
        out_specs=(pl.BlockSpec(memory_space=pl.ANY), pl.BlockSpec(memory_space=pl.ANY), vmem),
        scratch_shapes=[
            pltpu.VMEM(keys_values.shape, jnp.bfloat16),
            pltpu.VMEM(selection.shape, jnp.int32),
            pltpu.VMEM(pos_weight.shape, jnp.bfloat16),
            pltpu.VMEM(compress_weight.shape, jnp.bfloat16),
            pltpu.SemaphoreType.DMA((4,)),
            pltpu.VMEM((slots,) + selection.shape, jnp.int32),
            pltpu.VMEM((slots, BLOCK, GROUPS * PAIR), jnp.bfloat16),
            pltpu.VMEM((16, 128), jnp.bfloat16),
            dma, dma, dma, dma, dma, dma,
            pltpu.SemaphoreType.DMA,
            pltpu.SemaphoreType.DMA,
        ],
        compiler_params=pltpu.CompilerParams(
            collective_id=0, has_side_effects=True, vmem_limit_bytes=56 << 20),
    )(keys_values, selection, pos_weight, compress_weight)


def value_rows(high):
    lane = lax.broadcasted_iota(jnp.int32, high.shape, 1)
    return jnp.where(lane >= WIDE - HEAD_DIM, high.astype(jnp.float32), 1.0).astype(jnp.bfloat16)


def branch(query_rows, keys, values, biases):
    heads = query_rows.shape[0] // BLOCK
    scores = []
    for key, bias in zip(keys, biases):
        raw = lax.dot_general(query_rows, key, (((1,), (1,)), ((), ())), preferred_element_type=jnp.float32)
        scores.append((raw.reshape(heads, BLOCK, raw.shape[1]) + bias[None]).reshape(raw.shape))
    top = jnp.max(functools.reduce(jnp.maximum, scores), axis=1, keepdims=True)
    total = None
    for score, value in zip(scores, values):
        weights = jnp.exp2((score - top) * EXP2_SCALE).astype(jnp.bfloat16)
        part = jnp.dot(weights, value, preferred_element_type=jnp.float32)
        total = part if total is None else total + part
    return total


def attend(grp_count, seq_count, sel_ref, q_ref, kv_ref, pool_ref, prev_ref, sums_ref, gate_ref,
           out_ref, keys, values, near_keys, near_values, sums_keys, sums_values, rows, totals, picks, spots):
    slots = grp_count + seq_count
    grp = lax.axis_index("grp")
    seq = lax.axis_index("seq")
    g = pl.program_id(0)
    b = pl.program_id(1)
    run = grp * seq_count + seq
    row_block = run * 2 + b
    key_cols = pl.ds(pl.multiple_of(g * PAIR, 128), WIDE)
    value_cols = pl.ds(pl.multiple_of(g * PAIR + PAIR - WIDE, 128), WIDE)
    all_blocks = sums_ref.shape[1]

    @pl.when(b == 0)
    def _():
        def fill(slot, carry):
            keys[slot] = pool_ref[slot, :, key_cols]
            values[slot] = value_rows(pool_ref[slot, :, value_cols])
            return carry

        lax.fori_loop(0, seq, fill, 0)
        lax.fori_loop(seq_count, seq_count + grp, fill, 0)
        own = kv_ref[:, key_cols], value_rows(kv_ref[:, value_cols])
        for i in range(2):
            keys[slots + i] = own[0][i * BLOCK:(i + 1) * BLOCK]
            values[slots + i] = own[1][i * BLOCK:(i + 1) * BLOCK]
        before = prev_ref[:, key_cols]
        near_keys[0:WINDOW] = jnp.where(run > 0, before, jnp.zeros_like(before))
        before = value_rows(prev_ref[:, value_cols])
        near_values[0:WINDOW] = jnp.where(run > 0, before, jnp.zeros_like(before))
        near_keys[WINDOW:2 * WINDOW] = own[0]
        near_values[WINDOW:2 * WINDOW] = own[1]
        sums_keys[0:all_blocks] = sums_ref[0, :, 0:WIDE]
        sums_values[0:all_blocks] = value_rows(sums_ref[0, :, PAIR - WIDE:PAIR])
        pad = (SINK_ROWS, WIDE)
        sums_keys[all_blocks:all_blocks + SINK_ROWS] = jnp.zeros(pad, jnp.bfloat16)
        sums_values[all_blocks:all_blocks + SINK_ROWS] = value_rows(jnp.zeros(pad, jnp.bfloat16))

    seg_blocks = 2 * seq_count

    for i in range(TOP):
        picks[i] = slots + b
        spots[i] = FAR_POS

    def scan(i, count):
        block = sel_ref[b, g * TOP + i]
        segment = block // seg_blocks
        place = (block - segment * seg_blocks) // 2
        here = jnp.logical_and(segment == grp, place == seq)
        slot = jnp.where(here, slots + (block & 1), jnp.where(segment == grp, place, seq_count + segment))

        @pl.when(block >= 0)
        def _():
            picks[count] = slot
            spots[count] = block * BLOCK

        return count + jnp.where(block >= 0, 1, 0)

    count = lax.fori_loop(0, TOP, scan, jnp.int32(0))

    wide_lane = lax.broadcasted_iota(jnp.int32, (BLOCK, WIDE), 1)
    for h in range(GROUP_HEADS):
        start = (h // 2) * PAIR + (h % 2) * (PAIR - WIDE)
        part = q_ref[:, start:start + WIDE].astype(jnp.float32)
        if h % 2:
            part = pltpu.roll(part, HEAD_DIM, 1)
        rows[h * BLOCK:(h + 1) * BLOCK] = jnp.where(wide_lane < HEAD_DIM, part, 0.0).astype(jnp.bfloat16)

    token = row_block * BLOCK + lax.broadcasted_iota(jnp.int32, (BLOCK, 1), 0)

    def bias_of(allowed):
        return jnp.where(allowed, 0.0, NEG_FILL)

    key_pos = run * 2 * BLOCK - WINDOW + lax.broadcasted_iota(jnp.int32, (BLOCK, 2 * WINDOW), 1)
    near_bias = bias_of((key_pos <= token) & (key_pos > token - WINDOW) & (key_pos >= 0))
    block_id = lax.broadcasted_iota(jnp.int32, (BLOCK, all_blocks + SINK_ROWS), 1)
    sums_bias = bias_of(((block_id < all_blocks) & (block_id * BLOCK + BLOCK - 1 <= token))
                        | (block_id == all_blocks))

    for part in range(PARTS):
        at = slice(part * PART_ROWS, (part + 1) * PART_ROWS)
        totals[0, at] = branch(rows[at], [sums_keys[...]], [sums_values[...]], [sums_bias])
        totals[2, at] = branch(rows[at], [near_keys[...]], [near_values[...]], [near_bias])

    lane = lax.broadcasted_iota(jnp.int32, (BLOCK, CHUNK * BLOCK), 1)

    def selected(chunks):
        biases = []
        for c in range(chunks):
            base = jnp.full(lane.shape, spots[c * CHUNK], jnp.int32)
            for j in range(1, CHUNK):
                base = jnp.where(lane >= j * BLOCK, spots[c * CHUNK + j], base)
            biases.append(bias_of(base + (lane & (BLOCK - 1)) <= token))

        def take(ref):
            return [
                jnp.concatenate([ref[picks[c * CHUNK + j]] for j in range(CHUNK)], axis=0)
                for c in range(chunks)
            ]

        for part in range(PARTS):
            at = slice(part * PART_ROWS, (part + 1) * PART_ROWS)
            totals[1, at] = branch(rows[at], take(keys), take(values), biases)

    for chunks in range(1, TOP // CHUNK + 1):
        low = 0 if chunks == 1 else (chunks - 1) * CHUNK + 1

        @pl.when(jnp.logical_and(count >= low, count <= chunks * CHUNK))
        def _():
            selected(chunks)

    head_lane = lax.broadcasted_iota(jnp.int32, (BLOCK, HEADS), 1)
    ratios = []
    for i in range(3):
        below = jnp.ones((BLOCK, HEADS), jnp.float32)
        for h in range(GROUP_HEADS):
            below = jnp.where(head_lane == g * GROUP_HEADS + h, totals[i, h * BLOCK:(h + 1) * BLOCK, 0:HEADS], below)
        gate = 1.0 / (1.0 + jnp.exp(-gate_ref[i].astype(jnp.float32)))
        ratio = gate / below
        ratios.append(jnp.where(g == 0, ratio[:, 0:GROUP_HEADS], ratio[:, GROUP_HEADS:HEADS]))

    half_lane = lax.broadcasted_iota(jnp.int32, (BLOCK, 128), 1) < 64

    def mixed(h):
        at = slice(h * BLOCK, (h + 1) * BLOCK)
        return sum(totals[i, at] * ratios[i][:, h:h + 1] for i in range(3))

    for j in range(PAIRS):
        even = pltpu.roll(mixed(2 * j), HEAD_DIM, 1)
        odd = mixed(2 * j + 1)
        start = j * PAIR
        out_ref[:, start:start + 128] = even[:, 0:128].astype(jnp.bfloat16)
        out_ref[:, start + 128:start + 256] = jnp.where(
            half_lane, even[:, 128:256], odd[:, 0:128]).astype(jnp.bfloat16)
        out_ref[:, start + 256:start + 384] = odd[:, 128:256].astype(jnp.bfloat16)


def run_attend(selection, queries, keys_values, pool, prev, sums, gate_logits):
    grp_count = lax.axis_size("grp")
    seq_count = lax.axis_size("seq")
    slots = grp_count + seq_count
    all_blocks = sums.shape[1]

    def whole(x):
        return pl.BlockSpec(x.shape, lambda g, b, *_: (0,) * x.ndim)

    group_cols = GROUP_HEADS * HEAD_DIM
    return pl.pallas_call(
        functools.partial(attend, grp_count, seq_count),
        out_shape=jax.ShapeDtypeStruct(queries.shape, jnp.bfloat16),
        grid_spec=pltpu.PrefetchScalarGridSpec(
            num_scalar_prefetch=1,
            grid=(GROUPS, 2),
            in_specs=[
                pl.BlockSpec((BLOCK, group_cols), lambda g, b, *_: (b, g)),
                whole(keys_values), whole(pool), whole(prev),
                pl.BlockSpec((1, all_blocks, PAIR), lambda g, b, *_: (g, 0, 0)),
                pl.BlockSpec((3, BLOCK, HEADS), lambda g, b, *_: (0, b, 0)),
            ],
            out_specs=pl.BlockSpec((BLOCK, group_cols), lambda g, b, *_: (b, g)),
            scratch_shapes=[
                pltpu.VMEM((slots + 2, BLOCK, WIDE), jnp.bfloat16),
                pltpu.VMEM((slots + 2, BLOCK, WIDE), jnp.bfloat16),
                pltpu.VMEM((2 * WINDOW, WIDE), jnp.bfloat16),
                pltpu.VMEM((2 * WINDOW, WIDE), jnp.bfloat16),
                pltpu.VMEM((all_blocks + SINK_ROWS, WIDE), jnp.bfloat16),
                pltpu.VMEM((all_blocks + SINK_ROWS, WIDE), jnp.bfloat16),
                pltpu.VMEM((GROUP_HEADS * BLOCK, WIDE), jnp.bfloat16),
                pltpu.VMEM((3, GROUP_HEADS * BLOCK, WIDE), jnp.float32),
                pltpu.SMEM((TOP,), jnp.int32),
                pltpu.SMEM((TOP,), jnp.int32),
            ],
        ),
        compiler_params=pltpu.CompilerParams(vmem_limit_bytes=56 << 20),
    )(selection, queries, keys_values, pool, prev, sums, gate_logits)


def shards(queries, keys_values, selection, gate_logits, pos_weight, compress_weight):
    grp_count = lax.axis_size("grp")
    seq_count = lax.axis_size("seq")
    pool, prev, packed = run_exchange(keys_values, selection, pos_weight, compress_weight)
    sums = packed[:, :, :12].reshape(seq_count, grp_count, 3, 2, GROUPS, 128)
    sums = jnp.transpose(sums, (4, 1, 0, 3, 2, 5)).reshape(GROUPS, 2 * seq_count * grp_count, PAIR)
    return run_attend(selection, queries, keys_values, pool, prev, sums, gate_logits)


def solution(mesh):
    in_specs = (
        P(("grp", "seq"), None),
        P(("grp", "seq"), None),
        P(("grp", "seq"), None),
        P(None, ("grp", "seq"), None),
        P(),
        P(),
    )
    out_specs = P(("grp", "seq"), None)
    return jax.shard_map(shards, mesh=mesh, in_specs=in_specs, out_specs=out_specs, check_vma=False)
```

```python
import functools
import math

import jax
import jax.numpy as jnp
from jax import lax
from jax.experimental import pallas as pl
from jax.experimental.pallas import tpu as pltpu
from jax.sharding import PartitionSpec as P

HEAD_DIM = 192
GROUPS = 2
GROUP_HEADS = 16
HEADS = 32
BLOCK = 64
TOP = 16
WINDOW = 128
PAIR = 2 * HEAD_DIM
WIDE = 256
CHUNK = 4
PAIRS = GROUP_HEADS // 2
SINK_ROWS = 64
PARTS = 2
PART_ROWS = GROUP_HEADS * BLOCK // PARTS
NEG_FILL = -1e30
EXP2_SCALE = HEAD_DIM ** (-0.5) * math.log2(math.e)
FAR_POS = 1 << 30


def exchange(grp_count, seq_count, kv_in, sel_in, pos_in, map_in, pool_ref, prev_ref, sums_ref,
             kv_ref, sel_ref, pos_ref, map_ref, load_sems, lists, staged, mine, list_send, list_recv, data_send, data_recv, sum_send, sum_recv,
             prev_send, prev_recv):
    grp = lax.axis_index("grp")
    seq = lax.axis_index("seq")
    last = seq_count - 1
    first_block = (grp * seq_count + seq) * 2

    loads = [
        pltpu.make_async_copy(src, dst, load_sems.at[i])
        for i, (src, dst) in enumerate(
            ((sel_in, sel_ref), (kv_in, kv_ref), (pos_in, pos_ref), (map_in, map_ref)))
    ]
    for load in loads:
        load.start()

    barrier = pltpu.get_barrier_semaphore()

    def near(place):
        return (grp, place)

    def far(segment):
        return (segment, seq)

    def greet(where):
        pl.semaphore_signal(barrier, inc=1, device_id=where, device_id_type=pl.DeviceIdType.MESH)

    def each(low, high, body):
        def step(i, carry):
            body(i)
            return carry

        lax.fori_loop(low, high, step, 0)

    def others(count, me, body):
        each(0, me, body)
        each(me + 1, count, body)

    others(seq_count, seq, lambda i: greet(near(i)))
    others(grp_count, grp, lambda i: greet(far(i)))
    tail_out = jnp.logical_and(seq == last, grp < grp_count - 1)
    tail_in = jnp.logical_and(seq == 0, grp > 0)

    @pl.when(tail_out)
    def _():
        greet((grp + 1, 0))

    @pl.when(tail_in)
    def _():
        greet((grp - 1, last))

    extra = tail_out.astype(jnp.int32) + tail_in.astype(jnp.int32)
    pl.semaphore_wait(barrier, seq_count + grp_count - 2 + extra)
    for load in loads:
        load.wait()

    def remote(src, dst, send, recv, where):
        return pltpu.make_async_remote_copy(
            src_ref=src, dst_ref=dst, send_sem=send, recv_sem=recv, device_id=where,
            device_id_type=pl.DeviceIdType.MESH)

    def list_copy(theirs, own, where):
        return remote(sel_ref, lists.at[own], list_send.at[theirs], list_recv.at[own], where)

    each(0, grp, lambda i: list_copy(seq_count + i, seq_count + grp, far(i)).start())
    each(0, seq - 1, lambda i: list_copy(i, seq, near(i)).start())

    def prev_copy(where):
        return remote(kv_ref, prev_ref, prev_send, prev_recv, where)

    @pl.when(seq < last)
    def _():
        prev_copy((grp, seq + 1)).start()

    @pl.when(tail_out)
    def _():
        prev_copy((grp + 1, 0)).start()

    rows = []
    for b in range(2):
        for g in range(GROUPS):
            part = kv_ref[b * BLOCK:(b + 1) * BLOCK, g * PAIR:(g + 1) * PAIR].astype(jnp.float32)
            rows.append(jnp.sum(part * pos_ref[...].astype(jnp.float32), axis=0, keepdims=True))
    pooled = jnp.concatenate(rows + [jnp.zeros((4, PAIR), jnp.float32)], axis=0).astype(jnp.bfloat16)
    mapped = jnp.dot(pooled, map_ref[...], preferred_element_type=jnp.float32)
    packed = jnp.concatenate(
        [mapped[0:4, c * 128:(c + 1) * 128] for c in range(3)] + [jnp.zeros((4, 128), jnp.float32)], axis=0)
    mine[...] = packed.astype(jnp.bfloat16)
    sums_ref[seq, grp] = mine[...]

    def column_copy(theirs, own, where):
        return remote(mine, sums_ref.at[seq, grp], sum_send.at[theirs], sum_recv.at[own], where)

    others(grp_count, grp, lambda i: column_copy(seq_count + i, seq_count + grp, far(i)).start())

    def data_copy(theirs, own, where):
        return remote(staged.at[theirs], pool_ref.at[own], data_send.at[theirs], data_recv.at[own], where)

    def answer(slot, own, where):
        list_copy(slot, slot, where).wait_recv()
        hit = jnp.where(lists[slot] == first_block + 1, 1.0, 0.0)
        for g in range(GROUPS):
            second = jnp.max(hit[:, g * TOP:(g + 1) * TOP], axis=(0, 1), keepdims=True)
            cols = pl.ds(g * PAIR, PAIR)
            low = kv_ref[0:BLOCK, cols].astype(jnp.float32)
            high = kv_ref[BLOCK:2 * BLOCK, cols].astype(jnp.float32)
            pick = jnp.broadcast_to(second, (BLOCK, PAIR)) > 0.5
            staged[slot, :, cols] = jnp.where(pick, high, low).astype(jnp.bfloat16)
        data_copy(slot, own, where).start()

    each(grp + 1, grp_count, lambda i: answer(seq_count + i, seq_count + grp, far(i)))
    each(seq + 2, seq_count, lambda i: answer(i, seq, near(i)))

    others(grp_count, grp, lambda i: column_copy(seq_count + i, seq_count + i, far(i)).wait_recv())

    def row_copy(theirs, own, where):
        return remote(sums_ref.at[seq], sums_ref.at[own], sum_send.at[theirs], sum_recv.at[own], where)

    others(seq_count, seq, lambda i: row_copy(i, seq, near(i)).start())

    def row_wait(i):
        remote(sums_ref.at[seq], sums_ref.at[i], sum_send.at[i], sum_recv.at[i], near(i)).wait_recv()

    others(seq_count, seq, row_wait)

    each(0, grp, lambda i: data_copy(seq_count + i, seq_count + i, far(i)).wait_recv())
    each(0, seq - 1, lambda i: data_copy(i, i, near(i)).wait_recv())

    @pl.when(jnp.logical_or(seq > 0, grp > 0))
    def _():
        prev_copy(far(grp)).wait_recv()

    @pl.when(jnp.logical_or(seq < last, grp < grp_count - 1))
    def _():
        prev_copy(far(grp)).wait_send()

    each(0, grp, lambda i: list_copy(seq_count + i, seq_count + i, far(i)).wait_send())
    each(0, seq - 1, lambda i: list_copy(i, i, near(i)).wait_send())
    each(grp + 1, grp_count, lambda i: data_copy(seq_count + i, seq_count + i, far(i)).wait_send())
    each(seq + 2, seq_count, lambda i: data_copy(i, i, near(i)).wait_send())
    others(grp_count, grp, lambda i: column_copy(seq_count + i, seq_count + i, far(i)).wait_send())
    others(seq_count, seq, lambda i: row_copy(i, seq, near(i)).wait_send())


def run_exchange(keys_values, selection, pos_weight, compress_weight):
    grp_count = lax.axis_size("grp")
    seq_count = lax.axis_size("seq")
    slots = grp_count + seq_count
    vmem = pl.BlockSpec(memory_space=pltpu.VMEM)
    dma = pltpu.SemaphoreType.DMA((slots,))
    return pl.pallas_call(
        functools.partial(exchange, grp_count, seq_count),
        out_shape=(
            jax.ShapeDtypeStruct((slots, BLOCK, GROUPS * PAIR), jnp.bfloat16),
            jax.ShapeDtypeStruct(keys_values.shape, jnp.bfloat16),
            jax.ShapeDtypeStruct((seq_count, grp_count, 16, 128), jnp.bfloat16),
        ),
        in_specs=[pl.BlockSpec(memory_space=pl.ANY)] * 4,
        out_specs=(pl.BlockSpec(memory_space=pl.ANY), pl.BlockSpec(memory_space=pl.ANY), vmem),
        scratch_shapes=[
            pltpu.VMEM(keys_values.shape, jnp.bfloat16),
            pltpu.VMEM(selection.shape, jnp.int32),
            pltpu.VMEM(pos_weight.shape, jnp.bfloat16),
            pltpu.VMEM(compress_weight.shape, jnp.bfloat16),
            pltpu.SemaphoreType.DMA((4,)),
            pltpu.VMEM((slots,) + selection.shape, jnp.int32),
            pltpu.VMEM((slots, BLOCK, GROUPS * PAIR), jnp.bfloat16),
            pltpu.VMEM((16, 128), jnp.bfloat16),
            dma, dma, dma, dma, dma, dma,
            pltpu.SemaphoreType.DMA,
            pltpu.SemaphoreType.DMA,
        ],
        compiler_params=pltpu.CompilerParams(
            collective_id=0, has_side_effects=True, vmem_limit_bytes=56 << 20),
    )(keys_values, selection, pos_weight, compress_weight)


def value_rows(high):
    lane = lax.broadcasted_iota(jnp.int32, high.shape, 1)
    return jnp.where(lane >= WIDE - HEAD_DIM, high.astype(jnp.float32), 1.0).astype(jnp.bfloat16)


def branch(query_rows, keys, values, biases):
    heads = query_rows.shape[0] // BLOCK
    scores = []
    for key, bias in zip(keys, biases):
        raw = lax.dot_general(query_rows, key, (((1,), (1,)), ((), ())), preferred_element_type=jnp.float32)
        scores.append((raw.reshape(heads, BLOCK, raw.shape[1]) + bias[None]).reshape(raw.shape))
    top = jnp.max(functools.reduce(jnp.maximum, scores), axis=1, keepdims=True)
    total = None
    for score, value in zip(scores, values):
        weights = jnp.exp2((score - top) * EXP2_SCALE).astype(jnp.bfloat16)
        part = jnp.dot(weights, value, preferred_element_type=jnp.float32)
        total = part if total is None else total + part
    return total


def attend(grp_count, seq_count, sel_ref, q_ref, kv_ref, pool_ref, prev_ref, sums_ref, gate_ref,
           out_ref, keys, values, near_keys, near_values, sums_keys, sums_values, rows, totals,
           unpacked, opened, picks, spots):
    slots = grp_count + seq_count
    grp = lax.axis_index("grp")
    seq = lax.axis_index("seq")
    g = pl.program_id(0)
    b = pl.program_id(1)
    run = grp * seq_count + seq
    row_block = run * 2 + b
    key_cols = pl.ds(pl.multiple_of(g * PAIR, 128), WIDE)
    value_cols = pl.ds(pl.multiple_of(g * PAIR + PAIR - WIDE, 128), WIDE)
    runs = grp_count * seq_count
    all_blocks = 2 * runs

    @pl.when(jnp.logical_and(g == 0, b == 0))
    def _():
        for i in range(3):
            opened[i] = (1.0 / (1.0 + jnp.exp(-gate_ref[i].astype(jnp.float32)))).T

    @pl.when(b == 0)
    def _():
        def fill(slot, carry):
            keys[slot] = pool_ref[slot, :, key_cols]
            values[slot] = value_rows(pool_ref[slot, :, value_cols])
            return carry

        lax.fori_loop(0, seq - 1, fill, 0)
        lax.fori_loop(seq_count, seq_count + grp, fill, 0)
        own = kv_ref[:, key_cols], value_rows(kv_ref[:, value_cols])
        for i in range(2):
            keys[slots + i] = own[0][i * BLOCK:(i + 1) * BLOCK]
            values[slots + i] = own[1][i * BLOCK:(i + 1) * BLOCK]
        before = prev_ref[:, key_cols]
        before = jnp.where(run > 0, before, jnp.zeros_like(before))
        near_keys[0:WINDOW] = before
        after = value_rows(prev_ref[:, value_cols])
        after = jnp.where(run > 0, after, jnp.zeros_like(after))
        near_values[0:WINDOW] = after
        for i in range(2):
            keys[slots + 2 + i] = before[i * BLOCK:(i + 1) * BLOCK]
            values[slots + 2 + i] = after[i * BLOCK:(i + 1) * BLOCK]
        near_keys[WINDOW:2 * WINDOW] = own[0]
        near_values[WINDOW:2 * WINDOW] = own[1]
        unpacked[...] = sums_ref[...].reshape(runs * 16, 128).astype(jnp.float32)
        for half in range(2):
            thirds = [
                unpacked[pl.ds(c * 4 + half * GROUPS + g, runs, stride=16), :].astype(jnp.bfloat16)
                for c in range(3)
            ]
            at = slice(half * runs, (half + 1) * runs)
            sums_keys[at] = jnp.concatenate(thirds[0:2], axis=1)
            sums_values[at] = value_rows(jnp.concatenate(thirds[1:3], axis=1))
        pad = (SINK_ROWS, WIDE)
        sums_keys[all_blocks:all_blocks + SINK_ROWS] = jnp.zeros(pad, jnp.bfloat16)
        sums_values[all_blocks:all_blocks + SINK_ROWS] = value_rows(jnp.zeros(pad, jnp.bfloat16))

    seg_blocks = 2 * seq_count

    for i in range(TOP):
        picks[i] = slots + b
        spots[i] = FAR_POS

    def scan(i, count):
        block = sel_ref[b, g * TOP + i]
        segment = block // seg_blocks
        place = (block - segment * seg_blocks) // 2
        here = jnp.logical_and(segment == grp, place == seq)
        slot = jnp.where(here, slots + (block & 1), jnp.where(segment == grp, place, seq_count + segment))
        just_before = jnp.logical_and(segment == grp, place == seq - 1)
        slot = jnp.where(just_before, slots + 2 + (block & 1), slot)

        @pl.when(block >= 0)
        def _():
            picks[count] = slot
            spots[count] = block * BLOCK

        return count + jnp.where(block >= 0, 1, 0)

    count = lax.fori_loop(0, TOP, scan, jnp.int32(0))

    wide_lane = lax.broadcasted_iota(jnp.int32, (BLOCK, WIDE), 1)
    for h in range(GROUP_HEADS):
        start = (h // 2) * PAIR + (h % 2) * (PAIR - WIDE)
        part = q_ref[:, start:start + WIDE].astype(jnp.float32)
        if h % 2:
            part = pltpu.roll(part, HEAD_DIM, 1)
        rows[h * BLOCK:(h + 1) * BLOCK] = jnp.where(wide_lane < HEAD_DIM, part, 0.0).astype(jnp.bfloat16)

    token = row_block * BLOCK + lax.broadcasted_iota(jnp.int32, (BLOCK, 1), 0)

    def bias_of(allowed):
        return jnp.where(allowed, 0.0, NEG_FILL)

    key_pos = run * 2 * BLOCK - WINDOW + lax.broadcasted_iota(jnp.int32, (BLOCK, 2 * WINDOW), 1)
    near_bias = bias_of((key_pos <= token) & (key_pos > token - WINDOW) & (key_pos >= 0))
    column = lax.broadcasted_iota(jnp.int32, (BLOCK, all_blocks + SINK_ROWS), 1)
    half = jnp.where(column >= runs, 1, 0)
    member = column - half * runs
    place = member // grp_count
    block_id = ((member - place * grp_count) * seq_count + place) * 2 + half
    sums_bias = bias_of(((column < all_blocks) & (block_id * BLOCK + BLOCK - 1 <= token))
                        | (column == all_blocks))

    for part in range(PARTS):
        at = slice(part * PART_ROWS, (part + 1) * PART_ROWS)
        totals[0, at] = branch(rows[at], [sums_keys[...]], [sums_values[...]], [sums_bias])
        totals[2, at] = branch(rows[at], [near_keys[...]], [near_values[...]], [near_bias])

    lane = lax.broadcasted_iota(jnp.int32, (BLOCK, CHUNK * BLOCK), 1)

    def selected(chunks):
        biases = []
        for c in range(chunks):
            base = jnp.full(lane.shape, spots[c * CHUNK], jnp.int32)
            for j in range(1, CHUNK):
                base = jnp.where(lane >= j * BLOCK, spots[c * CHUNK + j], base)
            biases.append(bias_of(base + (lane & (BLOCK - 1)) <= token))

        def take(ref):
            return [
                jnp.concatenate([ref[picks[c * CHUNK + j]] for j in range(CHUNK)], axis=0)
                for c in range(chunks)
            ]

        for part in range(PARTS):
            at = slice(part * PART_ROWS, (part + 1) * PART_ROWS)
            totals[1, at] = branch(rows[at], take(keys), take(values), biases)

    for chunks in range(1, TOP // CHUNK + 1):
        low = 0 if chunks == 1 else (chunks - 1) * CHUNK + 1

        @pl.when(jnp.logical_and(count >= low, count <= chunks * CHUNK))
        def _():
            selected(chunks)

    head_lane = lax.broadcasted_iota(jnp.int32, (BLOCK, HEADS), 1)
    ratios = []
    for i in range(3):
        below = jnp.ones((BLOCK, HEADS), jnp.float32)
        for h in range(GROUP_HEADS):
            below = jnp.where(head_lane == g * GROUP_HEADS + h, totals[i, h * BLOCK:(h + 1) * BLOCK, 0:HEADS], below)
        ratio = opened[i, pl.ds(pl.multiple_of(b * BLOCK, BLOCK), BLOCK)] / below
        ratios.append(jnp.where(g == 0, ratio[:, 0:GROUP_HEADS], ratio[:, GROUP_HEADS:HEADS]))

    half_lane = lax.broadcasted_iota(jnp.int32, (BLOCK, 128), 1) < 64

    def mixed(h):
        at = slice(h * BLOCK, (h + 1) * BLOCK)
        return sum(totals[i, at] * ratios[i][:, h:h + 1] for i in range(3))

    for j in range(PAIRS):
        even = pltpu.roll(mixed(2 * j), HEAD_DIM, 1)
        odd = mixed(2 * j + 1)
        start = j * PAIR
        out_ref[:, start:start + 128] = even[:, 0:128].astype(jnp.bfloat16)
        out_ref[:, start + 128:start + 256] = jnp.where(
            half_lane, even[:, 128:256], odd[:, 0:128]).astype(jnp.bfloat16)
        out_ref[:, start + 256:start + 384] = odd[:, 128:256].astype(jnp.bfloat16)


def run_attend(selection, queries, keys_values, pool, prev, sums, gate_logits):
    grp_count = lax.axis_size("grp")
    seq_count = lax.axis_size("seq")
    slots = grp_count + seq_count
    all_blocks = 2 * grp_count * seq_count

    def whole(x):
        return pl.BlockSpec(x.shape, lambda g, b, *_: (0,) * x.ndim)

    group_cols = GROUP_HEADS * HEAD_DIM
    return pl.pallas_call(
        functools.partial(attend, grp_count, seq_count),
        out_shape=jax.ShapeDtypeStruct(queries.shape, jnp.bfloat16),
        grid_spec=pltpu.PrefetchScalarGridSpec(
            num_scalar_prefetch=1,
            grid=(GROUPS, 2),
            in_specs=[
                pl.BlockSpec((BLOCK, group_cols), lambda g, b, *_: (b, g)),
                whole(keys_values), whole(pool), whole(prev),
                whole(sums),
                whole(gate_logits),
            ],
            out_specs=pl.BlockSpec((BLOCK, group_cols), lambda g, b, *_: (b, g)),
            scratch_shapes=[
                pltpu.VMEM((slots + 4, BLOCK, WIDE), jnp.bfloat16),
                pltpu.VMEM((slots + 4, BLOCK, WIDE), jnp.bfloat16),
                pltpu.VMEM((2 * WINDOW, WIDE), jnp.bfloat16),
                pltpu.VMEM((2 * WINDOW, WIDE), jnp.bfloat16),
                pltpu.VMEM((all_blocks + SINK_ROWS, WIDE), jnp.bfloat16),
                pltpu.VMEM((all_blocks + SINK_ROWS, WIDE), jnp.bfloat16),
                pltpu.VMEM((GROUP_HEADS * BLOCK, WIDE), jnp.bfloat16),
                pltpu.VMEM((3, GROUP_HEADS * BLOCK, WIDE), jnp.float32),
                pltpu.VMEM((all_blocks * 8, 128), jnp.float32),
                pltpu.VMEM((3, 2 * BLOCK, HEADS), jnp.float32),
                pltpu.SMEM((TOP,), jnp.int32),
                pltpu.SMEM((TOP,), jnp.int32),
            ],
        ),
        compiler_params=pltpu.CompilerParams(vmem_limit_bytes=56 << 20),
    )(selection, queries, keys_values, pool, prev, sums, gate_logits)


def shards(queries, keys_values, selection, gate_logits, pos_weight, compress_weight):
    pool, prev, packed = run_exchange(keys_values, selection, pos_weight, compress_weight)
    return run_attend(
        selection, queries, keys_values, pool, prev, packed, jnp.transpose(gate_logits, (0, 2, 1)))


def solution(mesh):
    in_specs = (
        P(("grp", "seq"), None),
        P(("grp", "seq"), None),
        P(("grp", "seq"), None),
        P(None, ("grp", "seq"), None),
        P(),
        P(),
    )
    out_specs = P(("grp", "seq"), None)
    return jax.shard_map(shards, mesh=mesh, in_specs=in_specs, out_specs=out_specs, check_vma=False)
```

```python
import functools
import math

import jax
import jax.numpy as jnp
from jax import lax
from jax.experimental import pallas as pl
from jax.experimental.pallas import tpu as pltpu
from jax.sharding import PartitionSpec as P

HEAD_DIM = 192
GROUPS = 2
GROUP_HEADS = 16
HEADS = 32
BLOCK = 64
TOP = 16
WINDOW = 128
PAIR = 2 * HEAD_DIM
WIDE = 256
CHUNK = 4
PAIRS = GROUP_HEADS // 2
SINK_ROWS = 64
PARTS = 2
PART_ROWS = GROUP_HEADS * BLOCK // PARTS
NEG_FILL = -1e30
EXP2_SCALE = HEAD_DIM ** (-0.5) * math.log2(math.e)
FAR_POS = 1 << 30


def exchange(grp_count, seq_count, kv_in, sel_in, pos_in, map_in, pool_ref, prev_ref, sums_ref,
             kv_ref, sel_ref, pos_ref, map_ref, load_sems, lists, staged, mine, list_send, list_recv, data_send, data_recv, sum_send, sum_recv,
             prev_send, prev_recv):
    grp = lax.axis_index("grp")
    seq = lax.axis_index("seq")
    last = seq_count - 1
    first_block = (grp * seq_count + seq) * 2

    loads = [
        pltpu.make_async_copy(src, dst, load_sems.at[i])
        for i, (src, dst) in enumerate(
            ((sel_in, sel_ref), (kv_in, kv_ref), (pos_in, pos_ref), (map_in, map_ref)))
    ]
    for load in loads:
        load.start()

    barrier = pltpu.get_barrier_semaphore()

    def near(place):
        return (grp, place)

    def far(segment):
        return (segment, seq)

    def greet(where):
        pl.semaphore_signal(barrier, inc=1, device_id=where, device_id_type=pl.DeviceIdType.MESH)

    def each(low, high, body):
        def step(i, carry):
            body(i)
            return carry

        lax.fori_loop(low, high, step, 0)

    def others(count, me, body):
        each(0, me, body)
        each(me + 1, count, body)

    others(seq_count, seq, lambda i: greet(near(i)))
    others(grp_count, grp, lambda i: greet(far(i)))
    tail_out = jnp.logical_and(seq == last, grp < grp_count - 1)
    tail_in = jnp.logical_and(seq == 0, grp > 0)

    @pl.when(tail_out)
    def _():
        greet((grp + 1, 0))

    @pl.when(tail_in)
    def _():
        greet((grp - 1, last))

    extra = tail_out.astype(jnp.int32) + tail_in.astype(jnp.int32)
    pl.semaphore_wait(barrier, seq_count + grp_count - 2 + extra)
    for load in loads:
        load.wait()

    def remote(src, dst, send, recv, where):
        return pltpu.make_async_remote_copy(
            src_ref=src, dst_ref=dst, send_sem=send, recv_sem=recv, device_id=where,
            device_id_type=pl.DeviceIdType.MESH)

    def list_copy(theirs, own, where):
        return remote(sel_ref, lists.at[own], list_send.at[theirs], list_recv.at[own], where)

    each(0, grp, lambda i: list_copy(seq_count + i, seq_count + grp, far(i)).start())
    each(0, seq - 1, lambda i: list_copy(i, seq, near(i)).start())

    def prev_copy(where):
        return remote(kv_ref, prev_ref, prev_send, prev_recv, where)

    @pl.when(seq < last)
    def _():
        prev_copy((grp, seq + 1)).start()

    @pl.when(tail_out)
    def _():
        prev_copy((grp + 1, 0)).start()

    rows = []
    for b in range(2):
        for g in range(GROUPS):
            part = kv_ref[b * BLOCK:(b + 1) * BLOCK, g * PAIR:(g + 1) * PAIR].astype(jnp.float32)
            rows.append(jnp.sum(part * pos_ref[...].astype(jnp.float32), axis=0, keepdims=True))
    pooled = jnp.concatenate(rows + [jnp.zeros((4, PAIR), jnp.float32)], axis=0).astype(jnp.bfloat16)
    mapped = jnp.dot(pooled, map_ref[...], preferred_element_type=jnp.float32)
    packed = jnp.concatenate(
        [mapped[0:4, c * 128:(c + 1) * 128] for c in range(3)] + [jnp.zeros((4, 128), jnp.float32)], axis=0)
    mine[...] = packed.astype(jnp.bfloat16)
    sums_ref[seq, grp] = mine[...]

    def column_copy(theirs, own, where):
        return remote(mine, sums_ref.at[seq, grp], sum_send.at[theirs], sum_recv.at[own], where)

    others(grp_count, grp, lambda i: column_copy(seq_count + i, seq_count + grp, far(i)).start())

    def data_copy(theirs, own, where):
        return remote(staged.at[theirs], pool_ref.at[own], data_send.at[theirs], data_recv.at[own], where)

    def answer(slot, own, where):
        list_copy(slot, slot, where).wait_recv()
        hit = jnp.where(lists[slot] == first_block + 1, 1.0, 0.0)
        for g in range(GROUPS):
            second = jnp.max(hit[:, g * TOP:(g + 1) * TOP], axis=(0, 1), keepdims=True)
            cols = pl.ds(g * PAIR, PAIR)
            low = kv_ref[0:BLOCK, cols].astype(jnp.float32)
            high = kv_ref[BLOCK:2 * BLOCK, cols].astype(jnp.float32)
            pick = jnp.broadcast_to(second, (BLOCK, PAIR)) > 0.5
            staged[slot, :, cols] = jnp.where(pick, high, low).astype(jnp.bfloat16)
        data_copy(slot, own, where).start()

    each(grp + 1, grp_count, lambda i: answer(seq_count + i, seq_count + grp, far(i)))
    each(seq + 2, seq_count, lambda i: answer(i, seq, near(i)))

    others(grp_count, grp, lambda i: column_copy(seq_count + i, seq_count + i, far(i)).wait_recv())

    def row_copy(theirs, own, where):
        return remote(sums_ref.at[seq], sums_ref.at[own], sum_send.at[theirs], sum_recv.at[own], where)

    others(seq_count, seq, lambda i: row_copy(i, seq, near(i)).start())

    def row_wait(i):
        remote(sums_ref.at[seq], sums_ref.at[i], sum_send.at[i], sum_recv.at[i], near(i)).wait_recv()

    others(seq_count, seq, row_wait)

    each(0, grp, lambda i: data_copy(seq_count + i, seq_count + i, far(i)).wait_recv())
    each(0, seq - 1, lambda i: data_copy(i, i, near(i)).wait_recv())

    @pl.when(jnp.logical_or(seq > 0, grp > 0))
    def _():
        prev_copy(far(grp)).wait_recv()

    @pl.when(jnp.logical_or(seq < last, grp < grp_count - 1))
    def _():
        prev_copy(far(grp)).wait_send()

    each(0, grp, lambda i: list_copy(seq_count + i, seq_count + i, far(i)).wait_send())
    each(0, seq - 1, lambda i: list_copy(i, i, near(i)).wait_send())
    each(grp + 1, grp_count, lambda i: data_copy(seq_count + i, seq_count + i, far(i)).wait_send())
    each(seq + 2, seq_count, lambda i: data_copy(i, i, near(i)).wait_send())
    others(grp_count, grp, lambda i: column_copy(seq_count + i, seq_count + i, far(i)).wait_send())
    others(seq_count, seq, lambda i: row_copy(i, seq, near(i)).wait_send())


def run_exchange(keys_values, selection, pos_weight, compress_weight):
    grp_count = lax.axis_size("grp")
    seq_count = lax.axis_size("seq")
    slots = grp_count + seq_count
    vmem = pl.BlockSpec(memory_space=pltpu.VMEM)
    dma = pltpu.SemaphoreType.DMA((slots,))
    return pl.pallas_call(
        functools.partial(exchange, grp_count, seq_count),
        out_shape=(
            jax.ShapeDtypeStruct((slots, BLOCK, GROUPS * PAIR), jnp.bfloat16),
            jax.ShapeDtypeStruct(keys_values.shape, jnp.bfloat16),
            jax.ShapeDtypeStruct((seq_count, grp_count, 16, 128), jnp.bfloat16),
        ),
        in_specs=[pl.BlockSpec(memory_space=pl.ANY)] * 4,
        out_specs=(pl.BlockSpec(memory_space=pl.ANY), pl.BlockSpec(memory_space=pl.ANY), vmem),
        scratch_shapes=[
            pltpu.VMEM(keys_values.shape, jnp.bfloat16),
            pltpu.VMEM(selection.shape, jnp.int32),
            pltpu.VMEM(pos_weight.shape, jnp.bfloat16),
            pltpu.VMEM(compress_weight.shape, jnp.bfloat16),
            pltpu.SemaphoreType.DMA((4,)),
            pltpu.VMEM((slots,) + selection.shape, jnp.int32),
            pltpu.VMEM((slots, BLOCK, GROUPS * PAIR), jnp.bfloat16),
            pltpu.VMEM((16, 128), jnp.bfloat16),
            dma, dma, dma, dma, dma, dma,
            pltpu.SemaphoreType.DMA,
            pltpu.SemaphoreType.DMA,
        ],
        compiler_params=pltpu.CompilerParams(
            collective_id=0, has_side_effects=True, vmem_limit_bytes=56 << 20),
    )(keys_values, selection, pos_weight, compress_weight)


def value_rows(high):
    lane = lax.broadcasted_iota(jnp.int32, high.shape, 1)
    return jnp.where(lane >= WIDE - HEAD_DIM, high.astype(jnp.float32), 1.0).astype(jnp.bfloat16)


def branch(query_rows, keys, values, biases):
    heads = query_rows.shape[0] // BLOCK
    scores = []
    for key, bias in zip(keys, biases):
        raw = lax.dot_general(query_rows, key, (((1,), (1,)), ((), ())), preferred_element_type=jnp.float32)
        scores.append((raw.reshape(heads, BLOCK, raw.shape[1]) + bias[None]).reshape(raw.shape))
    top = jnp.max(functools.reduce(jnp.maximum, scores), axis=1, keepdims=True)
    total = None
    for score, value in zip(scores, values):
        weights = jnp.exp2((score - top) * EXP2_SCALE).astype(jnp.bfloat16)
        part = jnp.dot(weights, value, preferred_element_type=jnp.float32)
        total = part if total is None else total + part
    return total


def attend(grp_count, seq_count, sel_ref, q_ref, kv_ref, pool_ref, prev_ref, sums_ref, gate_ref,
           out_ref, keys, values, near_keys, near_values, sums_keys, sums_values, rows, totals,
           unpacked, opened, picks, spots):
    slots = grp_count + seq_count
    grp = lax.axis_index("grp")
    seq = lax.axis_index("seq")
    g = pl.program_id(0)
    b = pl.program_id(1)
    run = grp * seq_count + seq
    row_block = run * 2 + b
    key_cols = pl.ds(pl.multiple_of(g * PAIR, 128), WIDE)
    value_cols = pl.ds(pl.multiple_of(g * PAIR + PAIR - WIDE, 128), WIDE)
    runs = grp_count * seq_count
    all_blocks = 2 * runs

    @pl.when(jnp.logical_and(g == 0, b == 0))
    def _():
        for i in range(3):
            opened[i] = (1.0 / (1.0 + jnp.exp(-gate_ref[i].astype(jnp.float32)))).T

    @pl.when(b == 0)
    def _():
        def fill(slot, carry):
            keys[slot] = pool_ref[slot, :, key_cols]
            values[slot] = value_rows(pool_ref[slot, :, value_cols])
            return carry

        lax.fori_loop(0, seq - 1, fill, 0)
        lax.fori_loop(seq_count, seq_count + grp, fill, 0)
        own = kv_ref[:, key_cols], value_rows(kv_ref[:, value_cols])
        for i in range(2):
            keys[slots + i] = own[0][i * BLOCK:(i + 1) * BLOCK]
            values[slots + i] = own[1][i * BLOCK:(i + 1) * BLOCK]
        before = prev_ref[:, key_cols]
        before = jnp.where(run > 0, before, jnp.zeros_like(before))
        near_keys[0:WINDOW] = before
        after = value_rows(prev_ref[:, value_cols])
        after = jnp.where(run > 0, after, jnp.zeros_like(after))
        near_values[0:WINDOW] = after
        for i in range(2):
            keys[slots + 2 + i] = before[i * BLOCK:(i + 1) * BLOCK]
            values[slots + 2 + i] = after[i * BLOCK:(i + 1) * BLOCK]
        near_keys[WINDOW:2 * WINDOW] = own[0]
        near_values[WINDOW:2 * WINDOW] = own[1]
        unpacked[...] = sums_ref[...].reshape(runs * 16, 128).astype(jnp.float32)
        for half in range(2):
            thirds = [
                unpacked[pl.ds(c * 4 + half * GROUPS + g, runs, stride=16), :].astype(jnp.bfloat16)
                for c in range(3)
            ]
            at = slice(half * runs, (half + 1) * runs)
            sums_keys[at] = jnp.concatenate(thirds[0:2], axis=1)
            sums_values[at] = value_rows(jnp.concatenate(thirds[1:3], axis=1))
        pad = (SINK_ROWS, WIDE)
        sums_keys[all_blocks:all_blocks + SINK_ROWS] = jnp.zeros(pad, jnp.bfloat16)
        sums_values[all_blocks:all_blocks + SINK_ROWS] = value_rows(jnp.zeros(pad, jnp.bfloat16))

    seg_blocks = 2 * seq_count

    for i in range(TOP):
        picks[i] = slots + b
        spots[i] = FAR_POS

    def scan(i, count):
        block = sel_ref[b, g * TOP + i]
        segment = block // seg_blocks
        place = (block - segment * seg_blocks) // 2
        here = jnp.logical_and(segment == grp, place == seq)
        slot = jnp.where(here, slots + (block & 1), jnp.where(segment == grp, place, seq_count + segment))
        just_before = jnp.logical_and(segment == grp, place == seq - 1)
        slot = jnp.where(just_before, slots + 2 + (block & 1), slot)

        @pl.when(block >= 0)
        def _():
            picks[count] = slot
            spots[count] = block * BLOCK

        return count + jnp.where(block >= 0, 1, 0)

    count = lax.fori_loop(0, TOP, scan, jnp.int32(0))

    wide_lane = lax.broadcasted_iota(jnp.int32, (BLOCK, WIDE), 1)
    for h in range(GROUP_HEADS):
        start = (h // 2) * PAIR + (h % 2) * (PAIR - WIDE)
        part = q_ref[:, start:start + WIDE].astype(jnp.float32)
        if h % 2:
            part = pltpu.roll(part, HEAD_DIM, 1)
        rows[h * BLOCK:(h + 1) * BLOCK] = jnp.where(wide_lane < HEAD_DIM, part, 0.0).astype(jnp.bfloat16)

    token = row_block * BLOCK + lax.broadcasted_iota(jnp.int32, (BLOCK, 1), 0)

    def bias_of(allowed):
        return jnp.where(allowed, 0.0, NEG_FILL)

    key_pos = run * 2 * BLOCK - WINDOW + lax.broadcasted_iota(jnp.int32, (BLOCK, 2 * WINDOW), 1)
    near_bias = bias_of((key_pos <= token) & (key_pos > token - WINDOW) & (key_pos >= 0))
    column = lax.broadcasted_iota(jnp.int32, (BLOCK, all_blocks + SINK_ROWS), 1)
    half = jnp.where(column >= runs, 1, 0)
    member = column - half * runs
    place = member // grp_count
    block_id = ((member - place * grp_count) * seq_count + place) * 2 + half
    sums_bias = bias_of(((column < all_blocks) & (block_id * BLOCK + BLOCK - 1 <= token))
                        | (column == all_blocks))

    for part in range(PARTS):
        at = slice(part * PART_ROWS, (part + 1) * PART_ROWS)
        totals[0, at] = branch(rows[at], [sums_keys[...]], [sums_values[...]], [sums_bias])
        totals[2, at] = branch(rows[at], [near_keys[...]], [near_values[...]], [near_bias])

    lane = lax.broadcasted_iota(jnp.int32, (BLOCK, CHUNK * BLOCK), 1)

    def selected(chunks):
        biases = []
        for c in range(chunks):
            base = jnp.full(lane.shape, spots[c * CHUNK], jnp.int32)
            for j in range(1, CHUNK):
                base = jnp.where(lane >= j * BLOCK, spots[c * CHUNK + j], base)
            biases.append(bias_of(base + (lane & (BLOCK - 1)) <= token))

        def take(ref):
            return [
                jnp.concatenate([ref[picks[c * CHUNK + j]] for j in range(CHUNK)], axis=0)
                for c in range(chunks)
            ]

        for part in range(PARTS):
            at = slice(part * PART_ROWS, (part + 1) * PART_ROWS)
            totals[1, at] = branch(rows[at], take(keys), take(values), biases)

    for chunks in range(1, TOP // CHUNK + 1):
        low = 0 if chunks == 1 else (chunks - 1) * CHUNK + 1

        @pl.when(jnp.logical_and(count >= low, count <= chunks * CHUNK))
        def _():
            selected(chunks)

    head_lane = lax.broadcasted_iota(jnp.int32, (BLOCK, HEADS), 1)
    ratios = []
    for i in range(3):
        below = jnp.ones((BLOCK, HEADS), jnp.float32)
        for h in range(GROUP_HEADS):
            below = jnp.where(head_lane == g * GROUP_HEADS + h, totals[i, h * BLOCK:(h + 1) * BLOCK, 0:HEADS], below)
        ratio = opened[i, pl.ds(pl.multiple_of(b * BLOCK, BLOCK), BLOCK)] / below
        ratios.append(jnp.where(g == 0, ratio[:, 0:GROUP_HEADS], ratio[:, GROUP_HEADS:HEADS]))

    half_lane = lax.broadcasted_iota(jnp.int32, (BLOCK, 128), 1) < 64

    stacked = jnp.concatenate(ratios, axis=0)
    coarse = stacked.astype(jnp.bfloat16)
    fine = (stacked - coarse.astype(jnp.float32)).astype(jnp.bfloat16)
    source = lax.broadcasted_iota(jnp.int32, (GROUP_HEADS, GROUP_HEADS * 128), 0)
    target = lax.broadcasted_iota(jnp.int32, (GROUP_HEADS, GROUP_HEADS * 128), 1) // 128
    pattern = jnp.where(source == target, 1.0, 0.0).astype(jnp.bfloat16)
    spread = (jnp.dot(coarse, pattern, preferred_element_type=jnp.float32)
              + jnp.dot(fine, pattern, preferred_element_type=jnp.float32))

    def mixed(h):
        at = slice(h * BLOCK, (h + 1) * BLOCK)
        sides = [
            sum(totals[i, at, s:s + 128] * spread[i * BLOCK:(i + 1) * BLOCK, h * 128:(h + 1) * 128] for i in range(3))
            for s in (0, 128)
        ]
        return jnp.concatenate(sides, axis=1)

    for j in range(PAIRS):
        even = pltpu.roll(mixed(2 * j), HEAD_DIM, 1)
        odd = mixed(2 * j + 1)
        start = j * PAIR
        out_ref[:, start:start + 128] = even[:, 0:128].astype(jnp.bfloat16)
        out_ref[:, start + 128:start + 256] = jnp.where(
            half_lane, even[:, 128:256], odd[:, 0:128]).astype(jnp.bfloat16)
        out_ref[:, start + 256:start + 384] = odd[:, 128:256].astype(jnp.bfloat16)


def run_attend(selection, queries, keys_values, pool, prev, sums, gate_logits):
    grp_count = lax.axis_size("grp")
    seq_count = lax.axis_size("seq")
    slots = grp_count + seq_count
    all_blocks = 2 * grp_count * seq_count

    def whole(x):
        return pl.BlockSpec(x.shape, lambda g, b, *_: (0,) * x.ndim)

    group_cols = GROUP_HEADS * HEAD_DIM
    return pl.pallas_call(
        functools.partial(attend, grp_count, seq_count),
        out_shape=jax.ShapeDtypeStruct(queries.shape, jnp.bfloat16),
        grid_spec=pltpu.PrefetchScalarGridSpec(
            num_scalar_prefetch=1,
            grid=(GROUPS, 2),
            in_specs=[
                pl.BlockSpec((BLOCK, group_cols), lambda g, b, *_: (b, g)),
                whole(keys_values), whole(pool), whole(prev),
                whole(sums),
                whole(gate_logits),
            ],
            out_specs=pl.BlockSpec((BLOCK, group_cols), lambda g, b, *_: (b, g)),
            scratch_shapes=[
                pltpu.VMEM((slots + 4, BLOCK, WIDE), jnp.bfloat16),
                pltpu.VMEM((slots + 4, BLOCK, WIDE), jnp.bfloat16),
                pltpu.VMEM((2 * WINDOW, WIDE), jnp.bfloat16),
                pltpu.VMEM((2 * WINDOW, WIDE), jnp.bfloat16),
                pltpu.VMEM((all_blocks + SINK_ROWS, WIDE), jnp.bfloat16),
                pltpu.VMEM((all_blocks + SINK_ROWS, WIDE), jnp.bfloat16),
                pltpu.VMEM((GROUP_HEADS * BLOCK, WIDE), jnp.bfloat16),
                pltpu.VMEM((3, GROUP_HEADS * BLOCK, WIDE), jnp.float32),
                pltpu.VMEM((all_blocks * 8, 128), jnp.float32),
                pltpu.VMEM((3, 2 * BLOCK, HEADS), jnp.float32),
                pltpu.SMEM((TOP,), jnp.int32),
                pltpu.SMEM((TOP,), jnp.int32),
            ],
        ),
        compiler_params=pltpu.CompilerParams(vmem_limit_bytes=56 << 20),
    )(selection, queries, keys_values, pool, prev, sums, gate_logits)


def shards(queries, keys_values, selection, gate_logits, pos_weight, compress_weight):
    pool, prev, packed = run_exchange(keys_values, selection, pos_weight, compress_weight)
    return run_attend(
        selection, queries, keys_values, pool, prev, packed, jnp.transpose(gate_logits, (0, 2, 1)))


def solution(mesh):
    in_specs = (
        P(("grp", "seq"), None),
        P(("grp", "seq"), None),
        P(("grp", "seq"), None),
        P(None, ("grp", "seq"), None),
        P(),
        P(),
    )
    out_specs = P(("grp", "seq"), None)
    return jax.shard_map(shards, mesh=mesh, in_specs=in_specs, out_specs=out_specs, check_vma=False)
```
